32 devices in a mesh: group: 4 (over z), shard: 8 (over y, x, core).
Axes of the slice: x: 2, y: 2, z: 4, core: 2. Of those that a mesh axis runs over, the one named last changes fastest.
Arguments:
- vectors: float32 [4096, 256], P(('group', 'shard')), may hold values from -160 to 160
- item_codes: int32 [4096], P(('group', 'shard')), may hold values from 0 to 63, as said below
- coarse_book: float32 [64, 256], replicated, may hold values from -24 to 24
- fine_books: float32 [8, 16384, 256], P('group', 'shard'), may hold values from -2 to 2
Outputs:
- item_grad: float32 [4096, 256], P(('group', 'shard'))
- fine_grad: float32 [8, 16384, 256], P('group', 'shard')
- coarse_grad: float32 [64, 256], replicated
The draws below stay inside these ranges and needn't reach their ends.
Inputs may be any that keep to these rules, and one draw needn't show every extreme that they name: `item_codes`: the items of one device fall into one group at most 32 times, and one group receives exactly 32 items from every device.
All inputs are finite; a program needn't handle non-finite values.
Results may differ from the reference program's by a relative error of at most 0.0003.
Values sent between devices are 32-bit elements; how exact they have to be, the bound alone decides.
A program may use at most 192 MiB of HBM per device.

```python
import math
import jax
import jax.numpy as jnp
from jax import lax

D = 256
CODEBOOK = 16384
COARSE = 64
ITEM_DEV = 128
GROUPS = 8
SLOT = 32
ITEMS = 4096
N_GROUP = 4
N_SHARD = 8


def layout(key):
    key_star, key_rank, key_score, key_shuffle, key_code = jax.random.split(jax.random.fold_in(key, 7), 5)
    block_count = ITEMS // ITEM_DEV
    per_group = COARSE // GROUPS
    heavy_group = jax.random.randint(key_star, (), 0, GROUPS).astype(jnp.int32)
    ranking = jax.random.permutation(key_rank, GROUPS).astype(jnp.int32)
    others = (heavy_group + 1 + jnp.arange(GROUPS - 1, dtype=jnp.int32)) % GROUPS
    pooled = jnp.repeat(others, SLOT)
    pool_size = (GROUPS - 1) * SLOT
    jitter = jax.random.randint(key_score, (block_count, pool_size), 0, 4096)
    keyed = (jitter + ranking[pooled][None, :] * 256) * 4096 + jnp.arange(pool_size, dtype=jnp.int32)[None, :]
    picked = jnp.argsort(keyed, axis=1)[:, :ITEM_DEV - SLOT]
    chosen = pooled[picked].astype(jnp.int32)
    group_ids = jnp.concatenate([jnp.zeros((block_count, SLOT), jnp.int32) + heavy_group, chosen], 1)
    shuffle_keys = jax.random.randint(key_shuffle, (block_count, ITEM_DEV), 0, 65536) * ITEM_DEV + jnp.arange(ITEM_DEV, dtype=jnp.int32)[None, :]
    shuffle = jnp.argsort(shuffle_keys, axis=1)
    group_ids = jnp.take_along_axis(group_ids, shuffle, 1)
    within = jax.random.randint(key_code, (block_count, ITEM_DEV), 0, per_group)
    return (group_ids * per_group + within).reshape(ITEMS).astype(jnp.int32)


def coarse_draw(key):
    key_normal = jax.random.fold_in(jax.random.fold_in(key, 11), 0)
    standard = jnp.clip(jax.random.normal(key_normal, (COARSE, D), jnp.float32), -6.0, 6.0)
    return standard


def fine_draw(key):
    key_normal = jax.random.fold_in(jax.random.fold_in(key, 13), 0)
    standard = jnp.clip(jax.random.normal(key_normal, (GROUPS, CODEBOOK, D), jnp.float32), -6.0, 6.0)
    return standard / math.sqrt(D)


def draw_item_codes(key, part):
    return layout(key)


def draw_coarse_book(key, part):
    return coarse_draw(key)


def draw_fine_books(key, part):
    return fine_draw(key)


def draw_vectors(key, part):
    item_codes = layout(key)
    offset = coarse_draw(key)[item_codes]
    key_noise = jax.random.fold_in(jax.random.fold_in(key, 17), 0)
    drawn = jnp.clip(jax.random.normal(key_noise, (ITEMS, D), jnp.float32), -6.0, 6.0)
    return offset + drawn


def setup_inputs(seed: int = 0) -> dict:
    key_list = jax.random.split(jax.random.key(seed), 5)
    return {
        "vectors": draw_vectors(jax.random.fold_in(key_list[4], 71), 0),
        "item_codes": draw_item_codes(jax.random.fold_in(key_list[4], 71), 0),
        "coarse_book": draw_coarse_book(jax.random.fold_in(key_list[4], 71), 0),
        "fine_books": draw_fine_books(jax.random.fold_in(key_list[4], 71), 0),
    }


sharpness = 2.5
highest = lax.Precision.HIGHEST


def contract(former, latter, former_dim, latter_dim):
    return lax.dot_general(former, latter, (((former_dim,), (latter_dim,)), ((), ())), precision=highest, preferred_element_type=jnp.float32)


def reference(vectors, item_codes, coarse_book, fine_books):
    groups_all = fine_books.shape[0]
    per_group = COARSE // groups_all
    onehot = (item_codes[:, None] == jnp.arange(COARSE, dtype=jnp.int32)[None, :]).astype(jnp.float32)
    residual = vectors - contract(onehot, coarse_book, 1, 0)
    group_of = (item_codes // per_group).astype(jnp.int32)
    ordering = jnp.argsort(group_of, stable=True).astype(jnp.int32)
    sorted_rows = residual[ordering]
    sorted_group = group_of[ordering]
    counts = jnp.sum((group_of[:, None] == jnp.arange(groups_all, dtype=jnp.int32)[None, :]).astype(jnp.int32), axis=0)
    starts = (jnp.cumsum(counts) - counts).astype(jnp.int32)
    capacity = N_GROUP * N_SHARD * SLOT
    padded = jnp.concatenate([sorted_rows, jnp.zeros((capacity, D), jnp.float32)], 0)

    def one_group(group_index):
        first_row = starts[group_index]
        block_rows = lax.dynamic_slice_in_dim(padded, first_row, capacity, 0)
        live_mask = (jnp.arange(capacity, dtype=jnp.int32) < counts[group_index]).astype(jnp.float32)
        codebook = fine_books[group_index]
        scores = sharpness * contract(block_rows, codebook, 1, 1)
        peak_score = jnp.max(scores, axis=1)
        weights = jnp.exp(scores - peak_score[:, None])
        normalizer = jnp.sum(weights, axis=1)
        quantized = contract(weights, codebook, 1, 0) / normalizer[:, None]
        error_rows = (quantized - block_rows) * live_mask[:, None]
        inner_term = jnp.sum(error_rows * quantized, axis=1)
        probability = weights / normalizer[:, None]
        alignment = contract(error_rows, codebook, 1, 1)
        slopes = probability * (alignment - inner_term[:, None])
        grad_rows = sharpness * contract(slopes, codebook, 1, 0) - error_rows
        book_grad = contract(probability, error_rows, 0, 0) + sharpness * contract(slopes, block_rows, 0, 0)
        return grad_rows, book_grad

    grad_blocks, fine_grad = lax.map(one_group, jnp.arange(groups_all, dtype=jnp.int32))
    slot_of = (jnp.arange(ITEMS, dtype=jnp.int32) - starts[sorted_group]).astype(jnp.int32)
    grad_sorted = grad_blocks[sorted_group, slot_of]
    item_grad = jnp.zeros_like(vectors).at[ordering].set(grad_sorted)
    coarse_grad = -contract(onehot, item_grad, 0, 0)
    return item_grad, fine_grad, coarse_grad
```

```python
import functools

import jax
import jax.numpy as jnp
from jax import lax
from jax.experimental import pallas as pl
from jax.experimental.pallas import tpu as pltpu
from jax.sharding import PartitionSpec as P

sharpness = 2.5
highest = lax.Precision.HIGHEST
MESH = pl.DeviceIdType.MESH
VACANT = 4096.0
STAT = 8


def contract(former, latter, former_dim, latter_dim):
    return lax.dot_general(
        former,
        latter,
        (((former_dim,), (latter_dim,)), ((), ())),
        precision=highest,
        preferred_element_type=jnp.float32,
    )


def halves(value):
    high = value.astype(jnp.bfloat16)
    return high, (value - high.astype(jnp.float32)).astype(jnp.bfloat16)


def triple(former, latter, latter_dim):
    def one(left, right):
        return lax.dot_general(
            left,
            right,
            (((1,), (latter_dim,)), ((), ())),
            preferred_element_type=jnp.float32,
        )

    return (
        one(former[0], latter[0]) + one(former[0], latter[1]) + one(former[1], latter[0])
    )


def kernel(
    group_count,
    shard_count,
    slot,
    chunk,
    outgoing,
    books,
    home_out,
    fine_t,
    rows,
    book_high,
    book_low,
    weight_high,
    weight_low,
    scores,
    part_in,
    part_out,
    full,
    back,
    home,
    z_send,
    z_recv,
    ag_send,
    ag_recv,
    q_send,
    q_recv,
    f_send,
    f_recv,
    b_send,
    b_recv,
    h_send,
    h_recv,
):
    local_groups, book_rows, width = books.shape
    own = group_count * slot
    chips = shard_count // 2
    g = lax.axis_index("group")
    s = lax.axis_index("shard")
    chip = s // 2

    def shard_peer(offset):
        return lax.rem(s + offset, shard_count)

    def group_peer(offset):
        return lax.rem(g + offset, group_count)

    def remote(src, dst, send, recv, where):
        return pltpu.make_async_remote_copy(
            src_ref=src,
            dst_ref=dst,
            send_sem=send,
            recv_sem=recv,
            device_id=where,
            device_id_type=MESH,
        )

    barrier = pltpu.get_barrier_semaphore()
    for offset in range(1, group_count):
        pl.semaphore_signal(barrier, inc=1, device_id=(group_peer(offset), s), device_id_type=MESH)
    for offset in range(1, shard_count):
        pl.semaphore_signal(barrier, inc=1, device_id=(g, shard_peer(offset)), device_id_type=MESH)
    pl.semaphore_wait(barrier, group_count + shard_count - 2)

    def z_copy(b, other, landing):
        return remote(
            outgoing.at[b, other],
            rows.at[b, s, pl.ds(landing * slot, slot)],
            z_send.at[b, other],
            z_recv.at[b, landing],
            (other, s),
        )

    for b in range(local_groups):
        for offset in range(1, group_count):
            z_copy(b, group_peer(offset), g).start()
        rows[b, s, pl.ds(g * slot, slot)] = outgoing[b, g]

    def ag_copy(b, other, block):
        return remote(
            rows.at[b, block], rows.at[b, block], ag_send.at[b, other], ag_recv.at[b, block], (g, other)
        )

    def spread_rows(b):
        for offset in range(1, group_count):
            z_copy(b, group_peer(offset), group_peer(offset)).wait_recv()
        for offset in range(1, shard_count):
            other = shard_peer(offset)
            ag_copy(b, other, s).start()

    @pl.loop(0, book_rows // chunk)
    def _(step):
        at = pl.ds(step * chunk, chunk)
        for b in range(local_groups):
            high, low = halves(books[b, at])
            book_high[b, at] = high
            book_low[b, at] = low

    for b in range(local_groups):
        spread_rows(b)

    def load_rows(b, at, count):
        value = rows[b, at].reshape(count, width)
        live = (value[:, :1] < VACANT / 2).astype(jnp.float32)
        return value * live, live

    def book(b, step):
        at = pl.ds(step * chunk, chunk)
        return book_high[b, at], book_low[b, at]

    def q_copy(b, other, sender):
        return remote(
            part_out.at[b, other], part_in.at[b, sender], q_send.at[b, other], q_recv.at[b, sender], (g, other)
        )

    def b_copy(b, other, sender):
        return remote(
            part_out.at[b, other, pl.ds(0, own)],
            part_in.at[b, sender, pl.ds(0, own)],
            b_send.at[b, other],
            b_recv.at[b, sender],
            (g, other),
        )

    def f_copy(b, other, block):
        return remote(
            full.at[b, block], full.at[b, block], f_send.at[b, other], f_recv.at[b, block], (g, other)
        )

    steps = book_rows // chunk

    def score_tile(b, turn):
        tile = lax.rem(chip + turn, chips)
        for core in range(2):
            owner = 2 * tile + core

            @pl.when(owner != s)
            def _():
                ag_copy(b, owner, owner).wait_recv()

        entries, _ = load_rows(b, pl.ds(2 * tile, 2), 2 * own)
        pair = halves(entries)
        peak = None
        for step in range(steps):
            value = sharpness * triple(pair, book(b, step), 1)
            scores[:, step * chunk : (step + 1) * chunk] = value
            top = jnp.max(value, axis=1, keepdims=True)
            peak = top if peak is None else jnp.maximum(peak, top)
        total = jnp.zeros((2 * own, 1), jnp.float32)
        quant = jnp.zeros((2 * own, width), jnp.float32)
        for step in range(steps):
            weight = jnp.exp(scores[:, step * chunk : (step + 1) * chunk] - peak)
            total += jnp.sum(weight, axis=1, keepdims=True)
            high, low = halves(weight)
            weight_high[b, tile, :, step * chunk : (step + 1) * chunk] = high
            weight_low[b, tile, :, step * chunk : (step + 1) * chunk] = low
            quant += triple((high, low), book(b, step), 0)
        lane = lax.broadcasted_iota(jnp.int32, (2 * own, 128), 1)
        stats = jnp.where(lane == 0, peak, total)
        for core in range(2):
            owner = 2 * tile + core
            part_out[b, owner, :own] = quant[core * own : (core + 1) * own]
            part_out[b, owner, own:, :own] = stats[core * own : (core + 1) * own].T[:STAT]

            @pl.when(owner != s)
            def _():
                q_copy(b, owner, s).start()

    def combine(b):
        for offset in range(1, shard_count):
            q_copy(b, shard_peer(offset), shard_peer(offset)).wait_recv()
        part_in[b, s] = part_out[b, s]
        peaks = jnp.concatenate([part_in[b, i, own : own + 1, :own] for i in range(shard_count)], axis=0)
        totals = jnp.concatenate(
            [part_in[b, i, own + 1 : own + 2, :own] for i in range(shard_count)], axis=0
        )
        peak = jnp.max(peaks, axis=0, keepdims=True)
        factor = jnp.exp(peaks - peak)
        total = jnp.sum(factor * totals, axis=0, keepdims=True)
        factor_t = (factor / total).T
        value = jnp.zeros((own, width), jnp.float32)
        for i in range(shard_count):
            value += factor_t[:, i : i + 1] * part_in[b, i, :own]
        full[b, s, :own] = value
        line = lax.broadcasted_iota(jnp.int32, (STAT, own), 0)
        full[b, s, own:, :own] = jnp.where(line == 0, peak, 1.0 / total)
        for offset in range(1, shard_count):
            f_copy(b, shard_peer(offset), s).start()

    def slope_tile(b, turn):
        tile = lax.rem(chip + turn, chips)
        columns = []
        for core in range(2):
            owner = 2 * tile + core

            @pl.when(owner != s)
            def _():
                f_copy(b, owner, owner).wait_recv()
                q_copy(b, owner, s).wait_send()

            mine = part_out[b, owner, own:, :own]
            whole = full[b, owner, own:, :own]
            columns.append((jnp.exp(mine[:1] - whole[:1]) * whole[1:2] + jnp.zeros_like(mine)).T[:, :1])
        alpha = jnp.concatenate(columns, axis=0)
        entries, live = load_rows(b, pl.ds(2 * tile, 2), 2 * own)
        quantized = jnp.concatenate([full[b, 2 * tile, :own], full[b, 2 * tile + 1, :own]], axis=0)
        error = (quantized - entries) * live
        inner = jnp.sum(error * quantized, axis=1, keepdims=True)
        error_pair = halves(error)
        error_t = halves((alpha * error).T)
        entries_t = halves((sharpness * alpha * entries).T)
        pushed = jnp.zeros((2 * own, width), jnp.float32)
        for step in range(steps):
            at = slice(step * chunk, (step + 1) * chunk)
            align = triple(error_pair, book(b, step), 1)
            high = weight_high[b, tile, :, at]
            low = weight_low[b, tile, :, at]
            slope = (high.astype(jnp.float32) + low.astype(jnp.float32)) * (align - inner)
            slope_pair = halves(slope)
            pushed += triple(slope_pair, book(b, step), 0)
            fine_t[b, :, at] += triple(error_t, (high, low), 0) + triple(entries_t, slope_pair, 0)
        pushed = sharpness * alpha * pushed
        for core in range(2):
            owner = 2 * tile + core
            part_out[b, owner, :own] = pushed[core * own : (core + 1) * own]

            @pl.when(owner != s)
            def _():
                b_copy(b, owner, s).start()

    def h_copy(b, other, landing):
        return remote(
            back.at[b, other], home.at[b, landing], h_send.at[b, other], h_recv.at[b, landing], (other, s)
        )

    def finish(b):
        for offset in range(1, shard_count):
            b_copy(b, shard_peer(offset), shard_peer(offset)).wait_recv()
        entries, live = load_rows(b, pl.ds(s, 1), own)
        value = part_out[b, s, :own] - (full[b, s, :own] - entries) * live
        for offset in range(1, shard_count):
            value += part_in[b, shard_peer(offset), :own]
        back[b] = value.reshape(group_count, slot, width)
        for offset in range(1, group_count):
            h_copy(b, group_peer(offset), g).start()
        home[b, g] = back[b, g]

    def score_tiles(b, first, last):
        @pl.loop(first, last)
        def _(turn):
            score_tile(b, turn)

    def slope_tiles(b, first, last):
        @pl.loop(first, last)
        def _(turn):
            slope_tile(b, turn + 1)

    fine_t[...] = jnp.zeros_like(fine_t)
    half = chips // 2
    score_tiles(0, 0, chips)
    for b in range(1, local_groups):
        score_tiles(b, 0, half)
        combine(b - 1)
        score_tiles(b, half, chips)
    if local_groups == 1:
        combine(0)
    for b in range(local_groups):
        slope_tiles(b, 0, half)
        if b == 0 and local_groups > 1:
            combine(local_groups - 1)
        if b > 0:
            finish(b - 1)
        slope_tiles(b, half, chips)
    finish(local_groups - 1)
    for b in range(local_groups):
        for offset in range(1, group_count):
            h_copy(b, group_peer(offset), group_peer(offset)).wait_recv()
    home_out[...] = home[...]
    for b in range(local_groups):
        for offset in range(1, group_count):
            h_copy(b, group_peer(offset), g).wait_send()
            z_copy(b, group_peer(offset), g).wait_send()
        for offset in range(1, shard_count):
            other = shard_peer(offset)
            ag_copy(b, other, s).wait_send()
            f_copy(b, other, s).wait_send()
            b_copy(b, other, s).wait_send()


def per_device(vectors, item_codes, coarse_book, fine_books):
    local_groups, book_rows, width = fine_books.shape
    group_count = lax.axis_size("group")
    shard_count = lax.axis_size("shard")
    total_groups = local_groups * group_count
    coarse_total = coarse_book.shape[0]
    per_group = coarse_total // total_groups
    item_count = vectors.shape[0]
    slot = item_count // 4
    slot_total = total_groups * slot
    own = group_count * slot
    chunk = min(512, book_rows)
    onehot = (item_codes[:, None] == jnp.arange(coarse_total, dtype=jnp.int32)[None, :]).astype(
        jnp.float32
    )
    residual = vectors - contract(onehot, coarse_book, 1, 0)
    group_of = item_codes // per_group
    member = (group_of[:, None] == jnp.arange(total_groups, dtype=jnp.int32)[None, :]).astype(
        jnp.float32
    )
    index = jnp.arange(item_count, dtype=jnp.int32)
    earlier = (index[:, None] > index[None, :]).astype(jnp.float32)
    position = jnp.sum(contract(earlier, member, 1, 0) * member, axis=1).astype(jnp.int32)
    target = (
        group_of % local_groups * group_count + group_of // local_groups
    ) * slot + position
    placing = (jnp.arange(slot_total, dtype=jnp.int32)[:, None] == target[None, :]).astype(
        jnp.float32
    )
    vacant = VACANT * (1.0 - jnp.sum(placing, axis=1, keepdims=True))
    outgoing = (contract(placing, residual, 1, 0) + vacant).reshape(
        local_groups, group_count, slot, width
    )
    f32, bf16 = jnp.float32, jnp.bfloat16
    dma = pltpu.SemaphoreType.DMA
    message = (local_groups, shard_count, own + STAT, width)
    weights = (local_groups, shard_count // 2, 2 * own, book_rows)
    vmem = pl.BlockSpec(memory_space=pltpu.VMEM)
    home, fine_t = pl.pallas_call(
        functools.partial(kernel, group_count, shard_count, slot, chunk),
        out_shape=(
            jax.ShapeDtypeStruct((local_groups, group_count, slot, width), f32),
            jax.ShapeDtypeStruct((local_groups, width, book_rows), f32),
        ),
        in_specs=[vmem, vmem],
        out_specs=(vmem, vmem),
        scratch_shapes=[
            pltpu.VMEM((local_groups, shard_count, own, width), f32),
            pltpu.VMEM((local_groups, book_rows, width), bf16),
            pltpu.VMEM((local_groups, book_rows, width), bf16),
            pltpu.VMEM(weights, bf16),
            pltpu.VMEM(weights, bf16),
            pltpu.VMEM((2 * own, book_rows), f32),
            pltpu.VMEM(message, f32),
            pltpu.VMEM(message, f32),
            pltpu.VMEM(message, f32),
            pltpu.VMEM((local_groups, group_count, slot, width), f32),
            pltpu.VMEM((local_groups, group_count, slot, width), f32),
            dma((local_groups, group_count)),
            dma((local_groups, group_count)),
        ]
        + [dma((local_groups, shard_count)) for _ in range(8)]
        + [dma((local_groups, group_count)), dma((local_groups, group_count))],
        compiler_params=pltpu.CompilerParams(
            collective_id=0, has_side_effects=True, vmem_limit_bytes=62 * 1024 * 1024
        ),
    )(outgoing, fine_books)
    fine_grad = jnp.swapaxes(fine_t, 1, 2)
    item_grad = contract(placing, home.reshape(slot_total, width), 0, 0)
    coarse_grad = lax.psum(-contract(onehot, item_grad, 0, 0), ("group", "shard"))
    return (item_grad, fine_grad, coarse_grad)


def solution(mesh):
    placed = (P(("group", "shard"), None), P(("group", "shard")), P(), P("group", "shard", None))
    return jax.shard_map(
        per_device,
        mesh=mesh,
        in_specs=placed,
        out_specs=(P(("group", "shard"), None), P("group", "shard", None), P()),
        check_vma=False,
    )
```

```python
import functools

import jax
import jax.numpy as jnp
from jax import lax
from jax.experimental import pallas as pl
from jax.experimental.pallas import tpu as pltpu
from jax.sharding import PartitionSpec as P

sharpness = 2.5
highest = lax.Precision.HIGHEST
MESH = pl.DeviceIdType.MESH
VACANT = 4096.0
STAT = 8


def contract(former, latter, former_dim, latter_dim):
    return lax.dot_general(
        former,
        latter,
        (((former_dim,), (latter_dim,)), ((), ())),
        precision=highest,
        preferred_element_type=jnp.float32,
    )


def halves(value):
    high = value.astype(jnp.bfloat16)
    return high, (value - high.astype(jnp.float32)).astype(jnp.bfloat16)


def widened(left, right, latter_dim):
    return lax.dot_general(
        jnp.concatenate(left, axis=1),
        jnp.concatenate(right, axis=latter_dim),
        (((1,), (latter_dim,)), ((), ())),
        preferred_element_type=jnp.float32,
    )


def triple(former, latter, latter_dim):
    left = [former[0], former[0], former[1]]
    right = [latter[0], latter[1], latter[0]]
    return widened(left, right, latter_dim)


def kernel(
    group_count,
    shard_count,
    slot,
    chunk,
    outgoing,
    books,
    chooser,
    home_out,
    fine_t,
    coarse_out,
    rows,
    book_high,
    book_low,
    weight_high,
    weight_low,
    scores,
    part_in,
    part_out,
    full,
    back,
    home,
    coarse_part,
    coarse_in,
    coarse_mid,
    coarse_full,
    z_send,
    z_recv,
    ag_send,
    ag_recv,
    q_send,
    q_recv,
    f_send,
    f_recv,
    b_send,
    b_recv,
    h_send,
    h_recv,
    c_send,
    c_recv,
    m_send,
    m_recv,
    e_send,
    e_recv,
):
    local_groups, book_rows, width = books.shape
    own = group_count * slot
    chips = shard_count // 2
    g = lax.axis_index("group")
    s = lax.axis_index("shard")
    chip = s // 2

    def shard_peer(offset):
        return lax.rem(s + offset, shard_count)

    def group_peer(offset):
        return lax.rem(g + offset, group_count)

    def remote(src, dst, send, recv, where):
        return pltpu.make_async_remote_copy(
            src_ref=src,
            dst_ref=dst,
            send_sem=send,
            recv_sem=recv,
            device_id=where,
            device_id_type=MESH,
        )

    barrier = pltpu.get_barrier_semaphore()
    for offset in range(1, group_count):
        pl.semaphore_signal(barrier, inc=1, device_id=(group_peer(offset), s), device_id_type=MESH)
    for offset in range(1, shard_count):
        pl.semaphore_signal(barrier, inc=1, device_id=(g, shard_peer(offset)), device_id_type=MESH)
    pl.semaphore_wait(barrier, group_count + shard_count - 2)

    def z_copy(b, other, landing):
        return remote(
            outgoing.at[b, other],
            rows.at[b, s, pl.ds(landing * slot, slot)],
            z_send.at[b, other],
            z_recv.at[b, landing],
            (other, s),
        )

    for b in range(local_groups):
        for offset in range(1, group_count):
            z_copy(b, group_peer(offset), g).start()
        rows[b, s, pl.ds(g * slot, slot)] = outgoing[b, g]

    def ag_copy(b, other, block):
        return remote(
            rows.at[b, block], rows.at[b, block], ag_send.at[b, other], ag_recv.at[b, block], (g, other)
        )

    def spread_rows(b):
        for offset in range(1, group_count):
            z_copy(b, group_peer(offset), group_peer(offset)).wait_recv()
        for offset in range(1, shard_count):
            other = shard_peer(offset)
            ag_copy(b, other, s).start()

    def split_book(b):
        @pl.loop(0, book_rows // chunk)
        def _(step):
            at = pl.ds(step * chunk, chunk)
            high, low = halves(books[b, at])
            book_high[b, at] = high
            book_low[b, at] = low

    for b in range(local_groups):
        spread_rows(b)
        split_book(b)

    def load_rows(b, at, count):
        value = rows[b, at].reshape(count, width)
        live = (value[:, :1] < VACANT / 2).astype(jnp.float32)
        return value * live, live

    def book(b, step):
        at = pl.ds(step * chunk, chunk)
        return book_high[b, at], book_low[b, at]

    def q_copy(b, other, sender):
        return remote(
            part_out.at[b, other], part_in.at[b, sender], q_send.at[b, other], q_recv.at[b, sender], (g, other)
        )

    def b_copy(b, other, sender):
        return remote(
            part_out.at[b, other, pl.ds(0, own)],
            part_in.at[b, sender, pl.ds(0, own)],
            b_send.at[b, other],
            b_recv.at[b, sender],
            (g, other),
        )

    def f_copy(b, other, block):
        return remote(
            full.at[b, block], full.at[b, block], f_send.at[b, other], f_recv.at[b, block], (g, other)
        )

    steps = book_rows // chunk

    def score_tile(b, turn):
        tile = lax.rem(chip + turn, chips)
        for core in range(2):
            owner = 2 * tile + core

            @pl.when(owner != s)
            def _():
                ag_copy(b, owner, owner).wait_recv()

        entries, _ = load_rows(b, pl.ds(2 * tile, 2), 2 * own)
        pair = halves(entries)
        peak = None
        for step in range(steps):
            value = sharpness * triple(pair, book(b, step), 1)
            scores[:, step * chunk : (step + 1) * chunk] = value
            top = jnp.max(value, axis=1, keepdims=True)
            peak = top if peak is None else jnp.maximum(peak, top)
        total = jnp.zeros((2 * own, 1), jnp.float32)
        quant = jnp.zeros((2 * own, width), jnp.float32)
        for step in range(steps):
            weight = jnp.exp(scores[:, step * chunk : (step + 1) * chunk] - peak)
            total += jnp.sum(weight, axis=1, keepdims=True)
            high, low = halves(weight)
            weight_high[b, tile, :, step * chunk : (step + 1) * chunk] = high
            weight_low[b, tile, :, step * chunk : (step + 1) * chunk] = low
            quant += triple((high, low), book(b, step), 0)
        lane = lax.broadcasted_iota(jnp.int32, (2 * own, 128), 1)
        stats = jnp.where(lane == 0, peak, total)
        for core in range(2):
            owner = 2 * tile + core
            part_out[b, owner, :own] = quant[core * own : (core + 1) * own]
            part_out[b, owner, own:, :own] = stats[core * own : (core + 1) * own].T[:STAT]

            @pl.when(owner != s)
            def _():
                q_copy(b, owner, s).start()

    def combine(b):
        for offset in range(1, shard_count):
            q_copy(b, shard_peer(offset), shard_peer(offset)).wait_recv()
        part_in[b, s] = part_out[b, s]
        peaks = jnp.concatenate([part_in[b, i, own : own + 1, :own] for i in range(shard_count)], axis=0)
        totals = jnp.concatenate(
            [part_in[b, i, own + 1 : own + 2, :own] for i in range(shard_count)], axis=0
        )
        peak = jnp.max(peaks, axis=0, keepdims=True)
        factor = jnp.exp(peaks - peak)
        total = jnp.sum(factor * totals, axis=0, keepdims=True)
        factor_t = (factor / total).T
        value = jnp.zeros((own, width), jnp.float32)
        for i in range(shard_count):
            value += factor_t[:, i : i + 1] * part_in[b, i, :own]
        full[b, s, :own] = value
        line = lax.broadcasted_iota(jnp.int32, (STAT, own), 0)
        full[b, s, own:, :own] = jnp.where(line == 0, peak, 1.0 / total)
        for offset in range(1, shard_count):
            f_copy(b, shard_peer(offset), s).start()

    def slope_tile(b, turn):
        tile = lax.rem(chip + turn, chips)
        columns = []
        for core in range(2):
            owner = 2 * tile + core

            @pl.when(owner != s)
            def _():
                f_copy(b, owner, owner).wait_recv()
                q_copy(b, owner, s).wait_send()

            mine = part_out[b, owner, own:, :own]
            whole = full[b, owner, own:, :own]
            columns.append((jnp.exp(mine[:1] - whole[:1]) * whole[1:2] + jnp.zeros_like(mine)).T[:, :1])
        alpha = jnp.concatenate(columns, axis=0)
        entries, live = load_rows(b, pl.ds(2 * tile, 2), 2 * own)
        quantized = jnp.concatenate([full[b, 2 * tile, :own], full[b, 2 * tile + 1, :own]], axis=0)
        error = (quantized - entries) * live
        inner = jnp.sum(error * quantized, axis=1, keepdims=True)
        error_pair = halves(error)
        error_t = halves((alpha * error).T)
        entries_t = halves((sharpness * alpha * entries).T)
        pushed = jnp.zeros((2 * own, width), jnp.float32)
        for step in range(steps):
            at = slice(step * chunk, (step + 1) * chunk)
            align = triple(error_pair, book(b, step), 1)
            high = weight_high[b, tile, :, at]
            low = weight_low[b, tile, :, at]
            slope = (high.astype(jnp.float32) + low.astype(jnp.float32)) * (align - inner)
            slope_pair = halves(slope)
            pushed += triple(slope_pair, book(b, step), 0)
            fine_t[b, :, at] += widened(
                [error_t[0], error_t[0], error_t[1], entries_t[0], entries_t[0], entries_t[1]],
                [high, low, high, slope_pair[0], slope_pair[1], slope_pair[0]],
                0,
            )
        pushed = sharpness * alpha * pushed
        for core in range(2):
            owner = 2 * tile + core
            part_out[b, owner, :own] = pushed[core * own : (core + 1) * own]

            @pl.when(owner != s)
            def _():
                b_copy(b, owner, s).start()

    def h_copy(b, other, landing):
        return remote(
            back.at[b, other], home.at[b, landing], h_send.at[b, other], h_recv.at[b, landing], (other, s)
        )

    def finish(b):
        for offset in range(1, shard_count):
            b_copy(b, shard_peer(offset), shard_peer(offset)).wait_recv()
        entries, live = load_rows(b, pl.ds(s, 1), own)
        value = part_out[b, s, :own] - (full[b, s, :own] - entries) * live
        for offset in range(1, shard_count):
            value += part_in[b, shard_peer(offset), :own]
        back[b] = value.reshape(group_count, slot, width)
        for offset in range(1, group_count):
            h_copy(b, group_peer(offset), g).start()
        home[b, g] = back[b, g]

    def score_tiles(b, first, last):
        @pl.loop(first, last)
        def _(turn):
            score_tile(b, turn)

    def slope_tiles(b, first, last):
        @pl.loop(first, last)
        def _(turn):
            slope_tile(b, turn + 1)

    fine_t[...] = jnp.zeros_like(fine_t)
    half = chips // 2
    score_tiles(0, 0, chips)
    for b in range(1, local_groups):
        score_tiles(b, 0, half)
        combine(b - 1)
        score_tiles(b, half, chips)
    if local_groups == 1:
        combine(0)
    for b in range(local_groups):
        slope_tiles(b, 0, half)
        if b == 0 and local_groups > 1:
            combine(local_groups - 1)
        if b > 0:
            finish(b - 1)
        slope_tiles(b, half, chips)
    finish(local_groups - 1)
    for b in range(local_groups):
        for offset in range(1, group_count):
            h_copy(b, group_peer(offset), group_peer(offset)).wait_recv()
    home_out[...] = home[...]

    local = home[...].reshape(local_groups * own, width)
    select = chooser[...].astype(jnp.bfloat16)
    coarse = jnp.zeros((select.shape[0], width), jnp.float32)
    for _ in range(3):
        piece = local.astype(jnp.bfloat16)
        local = local - piece.astype(jnp.float32)
        coarse -= jnp.dot(select, piece, preferred_element_type=jnp.float32)
    count = coarse_part.shape[1]
    for i in range(shard_count):
        coarse_part[i] = coarse[i * count : (i + 1) * count]

    def c_copy(other, sender):
        return remote(
            coarse_part.at[other], coarse_in.at[sender], c_send.at[other], c_recv.at[sender], (g, other)
        )

    def m_copy(other, block):
        return remote(
            coarse_mid.at[block], coarse_mid.at[block], m_send.at[other], m_recv.at[block], (other, s)
        )

    def e_copy(other, block):
        return remote(
            coarse_full.at[block], coarse_full.at[block], e_send.at[other], e_recv.at[block], (g, other)
        )

    for offset in range(1, shard_count):
        c_copy(shard_peer(offset), s).start()
    coarse_in[s] = coarse_part[s]
    for offset in range(1, shard_count):
        c_copy(shard_peer(offset), shard_peer(offset)).wait_recv()
    coarse_mid[g] = jnp.sum(coarse_in[...], axis=0)
    for offset in range(1, group_count):
        m_copy(group_peer(offset), g).start()
    for offset in range(1, group_count):
        m_copy(group_peer(offset), group_peer(offset)).wait_recv()
    coarse_full[s] = jnp.sum(coarse_mid[...], axis=0)
    for offset in range(1, shard_count):
        e_copy(shard_peer(offset), s).start()
    for offset in range(1, shard_count):
        e_copy(shard_peer(offset), shard_peer(offset)).wait_recv()
    for i in range(shard_count):
        coarse_out[i * count : (i + 1) * count] = coarse_full[i]
    for offset in range(1, group_count):
        m_copy(group_peer(offset), g).wait_send()
    for offset in range(1, shard_count):
        c_copy(shard_peer(offset), s).wait_send()
        e_copy(shard_peer(offset), s).wait_send()
    for b in range(local_groups):
        for offset in range(1, group_count):
            h_copy(b, group_peer(offset), g).wait_send()
            z_copy(b, group_peer(offset), g).wait_send()
        for offset in range(1, shard_count):
            other = shard_peer(offset)
            ag_copy(b, other, s).wait_send()
            f_copy(b, other, s).wait_send()
            b_copy(b, other, s).wait_send()


def per_device(vectors, item_codes, coarse_book, fine_books):
    local_groups, book_rows, width = fine_books.shape
    group_count = lax.axis_size("group")
    shard_count = lax.axis_size("shard")
    total_groups = local_groups * group_count
    coarse_total = coarse_book.shape[0]
    per_group = coarse_total // total_groups
    item_count = vectors.shape[0]
    slot = item_count // 4
    slot_total = total_groups * slot
    own = group_count * slot
    chunk = min(512, book_rows)
    onehot = (item_codes[:, None] == jnp.arange(coarse_total, dtype=jnp.int32)[None, :]).astype(
        jnp.float32
    )
    residual = vectors - contract(onehot, coarse_book, 1, 0)
    group_of = item_codes // per_group
    member = (group_of[:, None] == jnp.arange(total_groups, dtype=jnp.int32)[None, :]).astype(
        jnp.float32
    )
    index = jnp.arange(item_count, dtype=jnp.int32)
    earlier = (index[:, None] > index[None, :]).astype(jnp.float32)
    position = jnp.sum(contract(earlier, member, 1, 0) * member, axis=1).astype(jnp.int32)
    target = (
        group_of % local_groups * group_count + group_of // local_groups
    ) * slot + position
    placing = (jnp.arange(slot_total, dtype=jnp.int32)[:, None] == target[None, :]).astype(
        jnp.float32
    )
    vacant = VACANT * (1.0 - jnp.sum(placing, axis=1, keepdims=True))
    outgoing = (contract(placing, residual, 1, 0) + vacant).reshape(
        local_groups, group_count, slot, width
    )
    f32, bf16 = jnp.float32, jnp.bfloat16
    dma = pltpu.SemaphoreType.DMA
    message = (local_groups, shard_count, own + STAT, width)
    weights = (local_groups, shard_count // 2, 2 * own, book_rows)
    vmem = pl.BlockSpec(memory_space=pltpu.VMEM)
    chooser = contract(onehot, placing, 0, 1)
    part = coarse_total // shard_count
    home, fine_t, coarse_grad = pl.pallas_call(
        functools.partial(kernel, group_count, shard_count, slot, chunk),
        out_shape=(
            jax.ShapeDtypeStruct((local_groups, group_count, slot, width), f32),
            jax.ShapeDtypeStruct((local_groups, width, book_rows), f32),
            jax.ShapeDtypeStruct((coarse_total, width), f32),
        ),
        in_specs=[vmem, vmem, vmem],
        out_specs=(vmem, vmem, vmem),
        scratch_shapes=[
            pltpu.VMEM((local_groups, shard_count, own, width), f32),
            pltpu.VMEM((local_groups, book_rows, width), bf16),
            pltpu.VMEM((local_groups, book_rows, width), bf16),
            pltpu.VMEM(weights, bf16),
            pltpu.VMEM(weights, bf16),
            pltpu.VMEM((2 * own, book_rows), f32),
            pltpu.VMEM(message, f32),
            pltpu.VMEM(message, f32),
            pltpu.VMEM(message, f32),
            pltpu.VMEM((local_groups, group_count, slot, width), f32),
            pltpu.VMEM((local_groups, group_count, slot, width), f32),
            pltpu.VMEM((shard_count, part, width), f32),
            pltpu.VMEM((shard_count, part, width), f32),
            pltpu.VMEM((group_count, part, width), f32),
            pltpu.VMEM((shard_count, part, width), f32),
            dma((local_groups, group_count)),
            dma((local_groups, group_count)),
        ]
        + [dma((local_groups, shard_count)) for _ in range(8)]
        + [dma((local_groups, group_count)) for _ in range(2)]
        + [dma((count,)) for count in [shard_count] * 2 + [group_count] * 2 + [shard_count] * 2],
        compiler_params=pltpu.CompilerParams(
            collective_id=0, has_side_effects=True, vmem_limit_bytes=62 * 1024 * 1024
        ),
    )(outgoing, fine_books, chooser)
    fine_grad = jnp.swapaxes(fine_t, 1, 2)
    item_grad = contract(placing, home.reshape(slot_total, width), 0, 0)
    return (item_grad, fine_grad, coarse_grad)


def solution(mesh):
    placed = (P(("group", "shard"), None), P(("group", "shard")), P(), P("group", "shard", None))
    return jax.shard_map(
        per_device,
        mesh=mesh,
        in_specs=placed,
        out_specs=(P(("group", "shard"), None), P("group", "shard", None), P()),
        check_vma=False,
    )
```

```python
import functools

import jax
import jax.numpy as jnp
from jax import lax
from jax.experimental import pallas as pl
from jax.experimental.pallas import tpu as pltpu
from jax.sharding import PartitionSpec as P

sharpness = 2.5
highest = lax.Precision.HIGHEST
MESH = pl.DeviceIdType.MESH
VACANT = 4096.0
STAT = 8


def contract(former, latter, former_dim, latter_dim):
    return lax.dot_general(
        former,
        latter,
        (((former_dim,), (latter_dim,)), ((), ())),
        precision=highest,
        preferred_element_type=jnp.float32,
    )


def halves(value):
    high = value.astype(jnp.bfloat16)
    return high, (value - high.astype(jnp.float32)).astype(jnp.bfloat16)


def widened(left, right, latter_dim):
    return lax.dot_general(
        jnp.concatenate(left, axis=1),
        jnp.concatenate(right, axis=latter_dim),
        (((1,), (latter_dim,)), ((), ())),
        preferred_element_type=jnp.float32,
    )


def triple(former, latter, latter_dim):
    left = [former[0], former[0], former[1]]
    right = [latter[0], latter[1], latter[0]]
    return widened(left, right, latter_dim)


def kernel(
    group_count,
    shard_count,
    slot,
    chunk,
    outgoing,
    books,
    chooser,
    home_out,
    fine_t,
    coarse_out,
    rows,
    book_high,
    book_low,
    weight_high,
    weight_low,
    scores,
    part_in,
    part_out,
    full,
    back,
    home,
    coarse_part,
    coarse_in,
    coarse_mid,
    coarse_full,
    z_send,
    z_recv,
    ag_send,
    ag_recv,
    q_send,
    q_recv,
    f_send,
    f_recv,
    b_send,
    b_recv,
    h_send,
    h_recv,
    c_send,
    c_recv,
    m_send,
    m_recv,
    e_send,
    e_recv,
):
    local_groups, book_rows, width = books.shape
    own = group_count * slot
    chips = shard_count // 2
    g = lax.axis_index("group")
    s = lax.axis_index("shard")
    chip = s // 2
    parity = lax.rem(s, 2)
    sibling = s + 1 - 2 * parity
    across = [lax.rem(s + 2 * hop, shard_count) for hop in range(1, chips)]

    def shard_peer(offset):
        return lax.rem(s + offset, shard_count)

    def group_peer(offset):
        return lax.rem(g + offset, group_count)

    def remote(src, dst, send, recv, where):
        return pltpu.make_async_remote_copy(
            src_ref=src,
            dst_ref=dst,
            send_sem=send,
            recv_sem=recv,
            device_id=where,
            device_id_type=MESH,
        )

    barrier = pltpu.get_barrier_semaphore()
    for offset in range(1, group_count):
        pl.semaphore_signal(barrier, inc=1, device_id=(group_peer(offset), s), device_id_type=MESH)
    for offset in range(1, shard_count):
        pl.semaphore_signal(barrier, inc=1, device_id=(g, shard_peer(offset)), device_id_type=MESH)
    pl.semaphore_wait(barrier, group_count + shard_count - 2)

    def z_copy(b, other, landing):
        return remote(
            outgoing.at[b, other],
            rows.at[b, s, pl.ds(landing * slot, slot)],
            z_send.at[b, other],
            z_recv.at[b, landing],
            (other, s),
        )

    for b in range(local_groups):
        for offset in range(1, group_count):
            z_copy(b, group_peer(offset), g).start()
        rows[b, s, pl.ds(g * slot, slot)] = outgoing[b, g]

    def ag_copy(b, other, block):
        return remote(
            rows.at[b, block], rows.at[b, block], ag_send.at[b, other], ag_recv.at[b, block], (g, other)
        )

    def passing(buffer, send, recv, b, block):
        return remote(
            buffer.at[b, block],
            buffer.at[b, block],
            send.at[b, block + 1 - 2 * parity],
            recv.at[b, block],
            (g, sibling),
        )

    def spread_rows(b):
        for offset in range(1, group_count):
            z_copy(b, group_peer(offset), group_peer(offset)).wait_recv()
        for other in across + [sibling]:
            ag_copy(b, other, s).start()

    def split_book(b):
        @pl.loop(0, book_rows // chunk)
        def _(step):
            at = pl.ds(step * chunk, chunk)
            high, low = halves(books[b, at])
            book_high[b, at] = high
            book_low[b, at] = low

    for b in range(local_groups):
        spread_rows(b)
        split_book(b)

    def load_rows(b, at, count):
        value = rows[b, at].reshape(count, width)
        live = (value[:, :1] < VACANT / 2).astype(jnp.float32)
        return value * live, live

    def book(b, step):
        at = pl.ds(step * chunk, chunk)
        return book_high[b, at], book_low[b, at]

    def q_copy(b, other, sender):
        return remote(
            part_out.at[b, other], part_in.at[b, sender], q_send.at[b, other], q_recv.at[b, sender], (g, other)
        )

    def b_copy(b, other, sender):
        return remote(
            part_out.at[b, other, pl.ds(0, own)],
            part_in.at[b, sender, pl.ds(0, own)],
            b_send.at[b, other],
            b_recv.at[b, sender],
            (g, other),
        )

    def f_copy(b, other, block):
        return remote(
            full.at[b, block], full.at[b, block], f_send.at[b, other], f_recv.at[b, block], (g, other)
        )

    steps = book_rows // chunk

    def score_tile(b, turn):
        tile = lax.rem(chip + turn, chips)
        other = 2 * tile + 1 - parity
        ag_copy(b, other, other).wait_recv()
        entries, _ = load_rows(b, pl.ds(2 * tile, 2), 2 * own)
        pair = halves(entries)
        peak = None
        for step in range(steps):
            value = sharpness * triple(pair, book(b, step), 1)
            scores[:, step * chunk : (step + 1) * chunk] = value
            top = jnp.max(value, axis=1, keepdims=True)
            peak = top if peak is None else jnp.maximum(peak, top)
        total = jnp.zeros((2 * own, 1), jnp.float32)
        quant = jnp.zeros((2 * own, width), jnp.float32)
        for step in range(steps):
            weight = jnp.exp(scores[:, step * chunk : (step + 1) * chunk] - peak)
            total += jnp.sum(weight, axis=1, keepdims=True)
            high, low = halves(weight)
            weight_high[b, tile, :, step * chunk : (step + 1) * chunk] = high
            weight_low[b, tile, :, step * chunk : (step + 1) * chunk] = low
            quant += triple((high, low), book(b, step), 0)
        lane = lax.broadcasted_iota(jnp.int32, (2 * own, 128), 1)
        stats = jnp.where(lane == 0, peak, total)
        for core in range(2):
            owner = 2 * tile + core
            part_out[b, owner, :own] = quant[core * own : (core + 1) * own]
            part_out[b, owner, own:, :own] = stats[core * own : (core + 1) * own].T[:STAT]

            @pl.when(owner != s)
            def _():
                q_copy(b, owner, s).start()

    def combine(b):
        for offset in range(1, shard_count):
            q_copy(b, shard_peer(offset), shard_peer(offset)).wait_recv()
        part_in[b, s] = part_out[b, s]
        peaks = jnp.concatenate([part_in[b, i, own : own + 1, :own] for i in range(shard_count)], axis=0)
        totals = jnp.concatenate(
            [part_in[b, i, own + 1 : own + 2, :own] for i in range(shard_count)], axis=0
        )
        peak = jnp.max(peaks, axis=0, keepdims=True)
        factor = jnp.exp(peaks - peak)
        total = jnp.sum(factor * totals, axis=0, keepdims=True)
        factor_t = (factor / total).T
        value = jnp.zeros((own, width), jnp.float32)
        for i in range(shard_count):
            value += factor_t[:, i : i + 1] * part_in[b, i, :own]
        full[b, s, :own] = value
        line = lax.broadcasted_iota(jnp.int32, (STAT, own), 0)
        full[b, s, own:, :own] = jnp.where(line == 0, peak, 1.0 / total)
        for other in across + [sibling]:
            f_copy(b, other, s).start()

    def slope_tile(b, turn):
        tile = lax.rem(chip + turn, chips)
        other = 2 * tile + 1 - parity
        f_copy(b, other, other).wait_recv()
        columns = []
        for core in range(2):
            owner = 2 * tile + core

            @pl.when(owner != s)
            def _():
                q_copy(b, owner, s).wait_send()

            mine = part_out[b, owner, own:, :own]
            whole = full[b, owner, own:, :own]
            columns.append((jnp.exp(mine[:1] - whole[:1]) * whole[1:2] + jnp.zeros_like(mine)).T[:, :1])
        alpha = jnp.concatenate(columns, axis=0)
        entries, live = load_rows(b, pl.ds(2 * tile, 2), 2 * own)
        quantized = jnp.concatenate([full[b, 2 * tile, :own], full[b, 2 * tile + 1, :own]], axis=0)
        error = (quantized - entries) * live
        inner = jnp.sum(error * quantized, axis=1, keepdims=True)
        error_pair = halves(error)
        error_t = halves((alpha * error).T)
        entries_t = halves((sharpness * alpha * entries).T)
        pushed = jnp.zeros((2 * own, width), jnp.float32)
        for step in range(steps):
            at = slice(step * chunk, (step + 1) * chunk)
            align = triple(error_pair, book(b, step), 1)
            high = weight_high[b, tile, :, at]
            low = weight_low[b, tile, :, at]
            slope = (high.astype(jnp.float32) + low.astype(jnp.float32)) * (align - inner)
            slope_pair = halves(slope)
            pushed += triple(slope_pair, book(b, step), 0)
            fine_t[b, :, at] += widened(
                [error_t[0], error_t[0], error_t[1], entries_t[0], entries_t[0], entries_t[1]],
                [high, low, high, slope_pair[0], slope_pair[1], slope_pair[0]],
                0,
            )
        pushed = sharpness * alpha * pushed
        for core in range(2):
            owner = 2 * tile + core
            part_out[b, owner, :own] = pushed[core * own : (core + 1) * own]

            @pl.when(owner != s)
            def _():
                b_copy(b, owner, s).start()

    def h_copy(b, other, landing):
        return remote(
            back.at[b, other], home.at[b, landing], h_send.at[b, other], h_recv.at[b, landing], (other, s)
        )

    def finish(b):
        for offset in range(1, shard_count):
            b_copy(b, shard_peer(offset), shard_peer(offset)).wait_recv()
        entries, live = load_rows(b, pl.ds(s, 1), own)
        value = part_out[b, s, :own] - (full[b, s, :own] - entries) * live
        for offset in range(1, shard_count):
            value += part_in[b, shard_peer(offset), :own]
        back[b] = value.reshape(group_count, slot, width)
        for offset in range(1, group_count):
            h_copy(b, group_peer(offset), g).start()
        home[b, g] = back[b, g]

    def score_tiles(b, first, last):
        @pl.loop(first, last)
        def _(turn):
            score_tile(b, turn)

    def slope_tiles(b, first, last):
        @pl.loop(first, last)
        def _(turn):
            slope_tile(b, turn + 1)

    def pass_rows(b):
        for block in across:
            ag_copy(b, block, block).wait_recv()
            passing(rows, ag_send, ag_recv, b, block).start()

    def pass_full(b):
        for block in across:
            f_copy(b, block, block).wait_recv()
            passing(full, f_send, f_recv, b, block).start()

    fine_t[...] = jnp.zeros_like(fine_t)
    half = chips // 2
    score_tiles(0, 0, 1)
    pass_rows(0)
    score_tiles(0, 1, chips)
    for b in range(1, local_groups):
        pass_rows(b)
        score_tiles(b, 0, half)
        combine(b - 1)
        score_tiles(b, half, chips)
    if local_groups == 1:
        combine(0)
    for b in range(local_groups):
        pass_full(b)
        slope_tiles(b, 0, half)
        if b == 0 and local_groups > 1:
            combine(local_groups - 1)
        if b > 0:
            finish(b - 1)
        slope_tiles(b, half, chips)
    finish(local_groups - 1)
    for b in range(local_groups):
        for offset in range(1, group_count):
            h_copy(b, group_peer(offset), group_peer(offset)).wait_recv()
    home_out[...] = home[...]

    local = home[...].reshape(local_groups * own, width)
    select = chooser[...].astype(jnp.bfloat16)
    coarse = jnp.zeros((select.shape[0], width), jnp.float32)
    for _ in range(3):
        piece = local.astype(jnp.bfloat16)
        local = local - piece.astype(jnp.float32)
        coarse -= jnp.dot(select, piece, preferred_element_type=jnp.float32)
    count = coarse_part.shape[1]
    for i in range(shard_count):
        coarse_part[i] = coarse[i * count : (i + 1) * count]

    def c_copy(other, sender):
        return remote(
            coarse_part.at[other], coarse_in.at[sender], c_send.at[other], c_recv.at[sender], (g, other)
        )

    def m_copy(other, block):
        return remote(
            coarse_mid.at[block], coarse_mid.at[block], m_send.at[other], m_recv.at[block], (other, s)
        )

    def e_copy(other, block):
        return remote(
            coarse_full.at[block], coarse_full.at[block], e_send.at[other], e_recv.at[block], (g, other)
        )

    for offset in range(1, shard_count):
        c_copy(shard_peer(offset), s).start()
    coarse_in[s] = coarse_part[s]
    for offset in range(1, shard_count):
        c_copy(shard_peer(offset), shard_peer(offset)).wait_recv()
    coarse_mid[g] = jnp.sum(coarse_in[...], axis=0)
    for offset in range(1, group_count):
        m_copy(group_peer(offset), g).start()
    for offset in range(1, group_count):
        m_copy(group_peer(offset), group_peer(offset)).wait_recv()
    coarse_full[s] = jnp.sum(coarse_mid[...], axis=0)
    for offset in range(1, shard_count):
        e_copy(shard_peer(offset), s).start()
    for offset in range(1, shard_count):
        e_copy(shard_peer(offset), shard_peer(offset)).wait_recv()
    for i in range(shard_count):
        coarse_out[i * count : (i + 1) * count] = coarse_full[i]
    for offset in range(1, group_count):
        m_copy(group_peer(offset), g).wait_send()
    for offset in range(1, shard_count):
        c_copy(shard_peer(offset), s).wait_send()
        e_copy(shard_peer(offset), s).wait_send()
    for b in range(local_groups):
        for offset in range(1, group_count):
            h_copy(b, group_peer(offset), g).wait_send()
            z_copy(b, group_peer(offset), g).wait_send()
        for offset in range(1, shard_count):
            b_copy(b, shard_peer(offset), s).wait_send()
        for other in across + [sibling]:
            ag_copy(b, other, s).wait_send()
            f_copy(b, other, s).wait_send()
        for block in across:
            passing(rows, ag_send, ag_recv, b, block).wait_send()
            passing(full, f_send, f_recv, b, block).wait_send()


def per_device(vectors, item_codes, coarse_book, fine_books):
    local_groups, book_rows, width = fine_books.shape
    group_count = lax.axis_size("group")
    shard_count = lax.axis_size("shard")
    total_groups = local_groups * group_count
    coarse_total = coarse_book.shape[0]
    per_group = coarse_total // total_groups
    item_count = vectors.shape[0]
    slot = item_count // 4
    slot_total = total_groups * slot
    own = group_count * slot
    chunk = min(512, book_rows)
    onehot = (item_codes[:, None] == jnp.arange(coarse_total, dtype=jnp.int32)[None, :]).astype(
        jnp.float32
    )
    residual = vectors - contract(onehot, coarse_book, 1, 0)
    group_of = item_codes // per_group
    member = (group_of[:, None] == jnp.arange(total_groups, dtype=jnp.int32)[None, :]).astype(
        jnp.float32
    )
    index = jnp.arange(item_count, dtype=jnp.int32)
    earlier = (index[:, None] > index[None, :]).astype(jnp.float32)
    position = jnp.sum(contract(earlier, member, 1, 0) * member, axis=1).astype(jnp.int32)
    target = (
        group_of % local_groups * group_count + group_of // local_groups
    ) * slot + position
    placing = (jnp.arange(slot_total, dtype=jnp.int32)[:, None] == target[None, :]).astype(
        jnp.float32
    )
    vacant = VACANT * (1.0 - jnp.sum(placing, axis=1, keepdims=True))
    outgoing = (contract(placing, residual, 1, 0) + vacant).reshape(
        local_groups, group_count, slot, width
    )
    f32, bf16 = jnp.float32, jnp.bfloat16
    dma = pltpu.SemaphoreType.DMA
    message = (local_groups, shard_count, own + STAT, width)
    weights = (local_groups, shard_count // 2, 2 * own, book_rows)
    vmem = pl.BlockSpec(memory_space=pltpu.VMEM)
    chooser = contract(onehot, placing, 0, 1)
    part = coarse_total // shard_count
    home, fine_t, coarse_grad = pl.pallas_call(
        functools.partial(kernel, group_count, shard_count, slot, chunk),
        out_shape=(
            jax.ShapeDtypeStruct((local_groups, group_count, slot, width), f32),
            jax.ShapeDtypeStruct((local_groups, width, book_rows), f32),
            jax.ShapeDtypeStruct((coarse_total, width), f32),
        ),
        in_specs=[vmem, vmem, vmem],
        out_specs=(vmem, vmem, vmem),
        scratch_shapes=[
            pltpu.VMEM((local_groups, shard_count, own, width), f32),
            pltpu.VMEM((local_groups, book_rows, width), bf16),
            pltpu.VMEM((local_groups, book_rows, width), bf16),
            pltpu.VMEM(weights, bf16),
            pltpu.VMEM(weights, bf16),
            pltpu.VMEM((2 * own, book_rows), f32),
            pltpu.VMEM(message, f32),
            pltpu.VMEM(message, f32),
            pltpu.VMEM(message, f32),
            pltpu.VMEM((local_groups, group_count, slot, width), f32),
            pltpu.VMEM((local_groups, group_count, slot, width), f32),
            pltpu.VMEM((shard_count, part, width), f32),
            pltpu.VMEM((shard_count, part, width), f32),
            pltpu.VMEM((group_count, part, width), f32),
            pltpu.VMEM((shard_count, part, width), f32),
            dma((local_groups, group_count)),
            dma((local_groups, group_count)),
        ]
        + [dma((local_groups, shard_count)) for _ in range(8)]
        + [dma((local_groups, group_count)) for _ in range(2)]
        + [dma((count,)) for count in [shard_count] * 2 + [group_count] * 2 + [shard_count] * 2],
        compiler_params=pltpu.CompilerParams(
            collective_id=0, has_side_effects=True, vmem_limit_bytes=62 * 1024 * 1024
        ),
    )(outgoing, fine_books, chooser)
    fine_grad = jnp.swapaxes(fine_t, 1, 2)
    item_grad = contract(placing, home.reshape(slot_total, width), 0, 0)
    return (item_grad, fine_grad, coarse_grad)


def solution(mesh):
    placed = (P(("group", "shard"), None), P(("group", "shard")), P(), P("group", "shard", None))
    return jax.shard_map(
        per_device,
        mesh=mesh,
        in_specs=placed,
        out_specs=(P(("group", "shard"), None), P("group", "shard", None), P()),
        check_vma=False,
    )
```
